32 devices in a mesh: leaf: 8 (over y, x, core), rank: 4 (over z).
Axes of the slice: x: 2, y: 2, z: 4, core: 2. Of those that a mesh axis runs over, the one named last changes fastest.
Arguments:
- load_vectors: bfloat16 [32, 4, 256], P('leaf'), may hold values from -6 to 6
- cluster_order: int32 [32, 256], P('leaf'), may hold values from 0 to 255, each once within a row
- block_present: int32 [8, 32], P(None, 'leaf'), may hold values 0 or 1
- factors: bfloat16 [8, 32, 2, 256, 256], P(None, 'leaf', None, 'rank'), may hold values from -0.25 to 0.25
Outputs:
- applied: float32 [32, 4, 256], P('leaf')
The draws below stay inside these ranges and needn't reach their ends.
Inputs may be any that keep to these rules, and one draw needn't show every extreme that they name: `cluster_order`: each row is a permutation of 0 .. 255.
All inputs are finite; a program needn't handle non-finite values. No bound on the sum of `block_present` on one device may be relied on, other than what follows from the above.
Results may differ from the reference program's by a relative error of at most 0.012.
Values may be sent and summed in bfloat16 or wider, within the bound.
A program may use at most 64 MiB of HBM per device.

```python
import jax
import jax.numpy as jnp
from jax import lax

B = 256
LOADS = 4
LEVELS = 8
BLOCKS = 32


def place_ends(result, stream_key, least, largest):
    extent = result.shape
    index_at = [jax.random.randint(jax.random.fold_in(stream_key, axis), (), 0, extent[axis]) for axis in range(len(extent))]
    result = result.at[tuple(index_at)].set(least)
    longest = extent.index(max(extent))
    index_at[longest] = (index_at[longest] + 1) % extent[longest]
    return result.at[tuple(index_at)].set(largest)


def levels(key, shape, cuts, smallest, largest):
    gain = 1.0
    for axis_at, parts in cuts:
        steps = jax.random.uniform(jax.random.fold_in(jax.random.fold_in(key, 6), axis_at), (parts,), jnp.float32, smallest / len(cuts), largest / len(cuts))
        gain = gain * jnp.repeat(jnp.exp(steps), shape[axis_at] // parts).reshape((-1,) + (1,) * (len(shape) - 1 - axis_at))
    return gain


def gaussian(rng, extent, spread, reach, shards=(), kind=jnp.bfloat16):
    gain = levels(rng, extent, shards, -0.22, 0.18) if shards else 1.0
    entries = jax.random.normal(rng, extent, jnp.float32) * spread * gain
    return jnp.minimum(jnp.maximum(entries, -reach), reach).astype(kind)


def setup_inputs(seed: int = 0) -> dict:
    seeds = jax.random.split(jax.random.key(seed), 5)
    load_vectors = gaussian(seeds[0], (BLOCKS, LOADS, B), 1.0, 6.0, ((0, 8),))
    cluster_order = jax.vmap(lambda own: jax.random.permutation(own, B))(jax.random.split(seeds[1], BLOCKS)).reshape((BLOCKS, B)).astype(jnp.int32)
    block_present = place_ends((jax.random.randint(seeds[2], (LEVELS, BLOCKS), 0, 4) < 3).astype(jnp.int32), jax.random.fold_in(seeds[2], 1), 0, 1)
    factors = gaussian(seeds[3], (LEVELS, BLOCKS, 2, B, B), (2 * B) ** -0.5, 0.25, ((1, 8), (3, 4)))
    return dict(load_vectors=load_vectors, cluster_order=cluster_order, block_present=block_present, factors=factors)


def reference(load_vectors, cluster_order, block_present, factors):
    current = jnp.take_along_axis(load_vectors, cluster_order[:, None, :], axis=2).astype(jnp.float32)
    tree_bits = BLOCKS.bit_length() - 1
    block_ids = jnp.arange(BLOCKS, dtype=jnp.int32)
    for level_idx in range(LEVELS):
        level_bit = (tree_bits - 1 - level_idx) % tree_bits
        rounded = lax.optimization_barrier(current.astype(jnp.bfloat16)).astype(jnp.float32)
        partner = rounded[block_ids ^ (1 << level_bit)]
        weights = factors[level_idx].astype(jnp.float32)
        own_term = jnp.einsum("blc,bco->blo", rounded, weights[:, 0], precision=lax.Precision.HIGHEST)
        off_term = jnp.einsum("blc,bco->blo", partner, weights[:, 1], precision=lax.Precision.HIGHEST)
        current = own_term + block_present[level_idx].astype(jnp.float32)[:, None, None] * off_term
    inverse = jnp.argsort(cluster_order, axis=1).astype(jnp.int32)
    return jnp.take_along_axis(current, inverse[:, None, :], axis=2)
```

```python
import functools

import jax
import jax.numpy as jnp
from jax import lax
from jax.experimental import pallas as pl
from jax.experimental.pallas import tpu as pltpu
from jax.sharding import PartitionSpec as P

MESH = pl.DeviceIdType.MESH


def kernel(
    leaves,
    ranks,
    loads_hbm,
    order_hbm,
    present_hbm,
    factors_hbm,
    out_ref,
    loads_ref,
    order_ref,
    present_ref,
    weights,
    last_weights,
    send,
    recv,
    last_send,
    last_recv,
    in_sem,
    weight_sem,
    send_sem,
    recv_sem,
    last_send_sem,
    last_recv_sem,
):
    levels, blocks, _, columns, width = factors_hbm.shape
    loads = loads_hbm.shape[1]
    half = blocks // 2
    rows = half * loads
    lanes = 2 * columns
    local_bits = blocks.bit_length() - 1
    tree_bits = local_bits + leaves.bit_length() - 1
    level_bits = [(tree_bits - 1 - level) % tree_bits for level in range(levels)]
    leaf = lax.axis_index("leaf")
    rank = lax.axis_index("rank")

    def partner_leaf(bit):
        step = 1 << (bit - local_bits)
        return leaf + step - 2 * step * ((leaf // step) % 2)

    def other_rank(away):
        return (rank + away) % ranks

    barrier = pltpu.get_barrier_semaphore()
    remote_bits = sorted({bit for bit in level_bits if bit >= local_bits})
    for away in range(1, ranks):
        pl.semaphore_signal(
            barrier, inc=1, device_id={"leaf": leaf, "rank": other_rank(away)}, device_id_type=MESH
        )
    for bit in remote_bits:
        for away in range(ranks):
            pl.semaphore_signal(
                barrier,
                inc=1,
                device_id={"leaf": partner_leaf(bit), "rank": other_rank(away)},
                device_id_type=MESH,
            )

    fetches = [
        pltpu.make_async_copy(order_hbm, order_ref, in_sem.at[0]),
        pltpu.make_async_copy(loads_hbm, loads_ref, in_sem.at[1]),
        pltpu.make_async_copy(present_hbm, present_ref, in_sem.at[2]),
    ]
    weight_fetches = [
        pltpu.make_async_copy(factors_hbm.at[level], weights.at[level], weight_sem.at[level])
        for level in range(levels)
    ]
    for fetch in fetches + weight_fetches:
        fetch.start()
    for fetch in fetches:
        fetch.wait()

    lane = lax.broadcasted_iota(jnp.int32, (rows, lanes), 1)
    row = lax.broadcasted_iota(jnp.int32, (rows, lanes), 0)
    left = lane < columns

    def picks(block):
        wanted = lax.broadcasted_iota(jnp.int32, (width, width), 0)
        return jnp.where(order_ref[pl.ds(block, 1), :] == wanted, 1.0, 0.0).astype(jnp.bfloat16)

    def gathered(block):
        return jnp.dot(loads_ref[block], picks(block), preferred_element_type=jnp.float32)

    def packed(upper, lower):
        own, partner = [], []
        for tile in range(ranks // 2):
            a = upper[:, tile * lanes : (tile + 1) * lanes]
            b = lower[:, tile * lanes : (tile + 1) * lanes]
            a_moved = pltpu.roll(a, columns, 1)
            b_moved = pltpu.roll(b, columns, 1)
            own += [jnp.where(left, a, b_moved), jnp.where(left, a_moved, b)]
            partner += [jnp.where(left, b, a_moved), jnp.where(left, b_moved, a)]
        return own, partner

    def present_mask(level):
        def rows_of(first):
            mask = jnp.zeros((rows, lanes), jnp.float32)
            for at in range(half):
                value = present_ref[level, first + at].astype(jnp.float32)
                mask = jnp.where(row // loads == at, value, mask)
            return mask

        return jnp.where(left, rows_of(half), rows_of(0))

    def remote(level, src, slot, to_leaf, to_rank):
        return pltpu.make_async_remote_copy(
            src_ref=src,
            dst_ref=recv.at[level, slot],
            send_sem=send_sem.at[level],
            recv_sem=recv_sem.at[level],
            device_id={"leaf": to_leaf, "rank": to_rank},
            device_id_type=MESH,
        )

    sent = [0] * levels

    first = [gathered(block) for block in range(blocks)]
    own, partner = packed(
        jnp.concatenate(first[:half], axis=0), jnp.concatenate(first[half:], axis=0)
    )
    for at in range(ranks):
        send[0, 0, at] = own[at]
        send[0, 1, at] = partner[at]
    pl.semaphore_wait(barrier, ranks - 1 + len(remote_bits) * ranks)
    if level_bits[0] >= local_bits:
        remote(0, send.at[0, 1, rank], ranks, partner_leaf(level_bits[0]), rank).start()
        sent[0] = 1

    for level in range(levels):
        bit = level_bits[level]
        mask = present_mask(level)
        if level == min(1, levels - 1):
            weight_fetches[levels - 1].wait()
            for block in range(blocks):
                wanted = picks(block)
                for side in range(2):
                    last_weights[block, side] = lax.dot_general(
                        weights[levels - 1, block, side],
                        wanted,
                        (((1,), (1,)), ((), ())),
                        preferred_element_type=jnp.float32,
                    ).astype(jnp.bfloat16)
        if level < levels - 1:
            weight_fetches[level].wait()
        if sent[level]:
            arrived = recv.at[level, pl.ds(0, sent[level])]
            pltpu.make_async_copy(arrived, arrived, recv_sem.at[level]).wait()
        if level == 0:
            state = send[0, 0, rank]
        else:
            state = recv[level, 0]
            for at in range(1, ranks):
                state = state + recv[level, at]
        if bit >= local_bits:
            other = recv[level, ranks]
            if level > 0:
                for at in range(1, ranks):
                    other = other + recv[level, ranks + at]
        elif bit == local_bits - 1:
            other = state
        else:
            away = loads << bit
            moved = pltpu.roll(state, columns, 1)
            other = jnp.where(
                (row // away) % 2 == 0,
                pltpu.roll(moved, rows - away, 0),
                pltpu.roll(moved, away, 0),
            )
        other = other * mask
        upper = jnp.where(left, state, other)
        lower = jnp.where(left, other, state)

        def spread(piece):
            return jnp.concatenate(
                [jnp.where(row // loads == at, piece, 0.0) for at in range(half)], axis=1
            ).astype(jnp.bfloat16)

        table = weights.at[level] if level < levels - 1 else last_weights
        upper_weights = [table[at, side] for at in range(half) for side in (0, 1)]
        lower_weights = [table[half + at, side] for at in range(half) for side in (1, 0)]
        upper = jnp.dot(
            spread(upper),
            jnp.concatenate(upper_weights, axis=0),
            preferred_element_type=jnp.float32,
        )
        lower = jnp.dot(
            spread(lower),
            jnp.concatenate(lower_weights, axis=0),
            preferred_element_type=jnp.float32,
        )
        if level == levels - 1:
            break
        own, partner = packed(upper, lower)
        then = level + 1
        with_partner = level_bits[then] >= local_bits
        for at in range(ranks):
            send[then, 0, at] = own[at]
            if with_partner:
                send[then, 1, at] = partner[at]
        for away in range(1, ranks):
            to = other_rank(away)
            remote(then, send.at[then, 0, to], rank, leaf, to).start()
            if with_partner:
                remote(
                    then, send.at[then, 1, to], ranks + rank, partner_leaf(level_bits[then]), to
                ).start()
        if with_partner:
            remote(
                then, send.at[then, 1, rank], ranks + rank, partner_leaf(level_bits[then]), rank
            ).start()
        sent[then] = ranks - 1 + (ranks if with_partner else 0)
        recv[then, rank] = send[then, 0, rank]

    last_send[...] = jnp.concatenate([upper, lower], axis=0).astype(jnp.bfloat16)
    lasts = [
        pltpu.make_async_remote_copy(
            src_ref=last_send,
            dst_ref=last_recv.at[rank],
            send_sem=last_send_sem,
            recv_sem=last_recv_sem,
            device_id={"leaf": leaf, "rank": other_rank(away)},
            device_id_type=MESH,
        )
        for away in range(1, ranks)
    ]
    for copy in lasts:
        copy.start()
    last_recv[rank] = last_send[...]
    for level in range(levels):
        if sent[level]:
            gone = recv.at[level, pl.ds(0, sent[level])]
            pltpu.make_async_copy(gone, gone, send_sem.at[level]).wait()
    arrived = last_recv.at[pl.ds(0, ranks - 1)]
    pltpu.make_async_copy(arrived, arrived, last_recv_sem).wait()
    total = last_recv[0].astype(jnp.float32)
    for at in range(1, ranks):
        total = total + last_recv[at].astype(jnp.float32)
    for block in range(blocks):
        out_ref[block] = total[block * loads : (block + 1) * loads]
    pltpu.make_async_copy(arrived, arrived, last_send_sem).wait()


def local(leaves, ranks, load_vectors, cluster_order, block_present, factors):
    levels, blocks, _, columns, width = factors.shape
    loads = load_vectors.shape[1]
    rows = blocks // 2 * loads
    lanes = 2 * columns
    return pl.pallas_call(
        functools.partial(kernel, leaves, ranks),
        out_shape=jax.ShapeDtypeStruct((blocks, loads, width), jnp.float32),
        in_specs=[pl.BlockSpec(memory_space=pl.ANY)] * 4,
        out_specs=pl.BlockSpec(memory_space=pltpu.VMEM),
        scratch_shapes=[
            pltpu.VMEM(load_vectors.shape, load_vectors.dtype),
            pltpu.VMEM(cluster_order.shape, cluster_order.dtype),
            pltpu.SMEM(block_present.shape, block_present.dtype),
            pltpu.VMEM(factors.shape, factors.dtype),
            pltpu.VMEM(factors.shape[1:], factors.dtype),
            pltpu.VMEM((levels, 2, ranks, rows, lanes), jnp.float32),
            pltpu.VMEM((levels, 2 * ranks, rows, lanes), jnp.float32),
            pltpu.VMEM((blocks * loads, width), jnp.bfloat16),
            pltpu.VMEM((ranks, blocks * loads, width), jnp.bfloat16),
            pltpu.SemaphoreType.DMA((3,)),
            pltpu.SemaphoreType.DMA((levels,)),
            pltpu.SemaphoreType.DMA((levels,)),
            pltpu.SemaphoreType.DMA((levels,)),
            pltpu.SemaphoreType.DMA,
            pltpu.SemaphoreType.DMA,
        ],
        compiler_params=pltpu.CompilerParams(
            collective_id=0, has_side_effects=True, vmem_limit_bytes=32 * 1024 * 1024
        ),
    )(load_vectors, cluster_order, block_present, factors)


def solution(mesh):
    in_specs = (
        P("leaf", None, None),
        P("leaf", None),
        P(None, "leaf"),
        P(None, "leaf", None, "rank", None),
    )
    return jax.shard_map(
        functools.partial(local, mesh.shape["leaf"], mesh.shape["rank"]),
        mesh=mesh,
        in_specs=in_specs,
        out_specs=P("leaf", None, None),
        check_vma=False,
    )
```

```python
import functools

import jax
import jax.numpy as jnp
from jax import lax
from jax.experimental import pallas as pl
from jax.experimental.pallas import tpu as pltpu
from jax.sharding import PartitionSpec as P

MESH = pl.DeviceIdType.MESH
VMEM_LIMIT = 63 * 1024 * 1024


def whole_level(level_bits, local_bits):
    for level in range(1, len(level_bits) - 2):
        if level_bits[level] == local_bits - 1 and level_bits[level + 1] < local_bits:
            return level
    return -1


def kernel(
    leaves,
    ranks,
    loads_hbm,
    order_hbm,
    present_hbm,
    factors_hbm,
    out_ref,
    loads_ref,
    order_ref,
    present_ref,
    weights,
    last_weights,
    send,
    recv,
    last_send,
    last_recv,
    whole_send,
    whole_recv,
    bulk_send,
    bulk_recv,
    in_sem,
    weight_sem,
    send_sem,
    recv_sem,
    last_send_sem,
    last_recv_sem,
    whole_sem,
    bulk_sem,
):
    levels, blocks, _, columns, width = factors_hbm.shape
    loads = loads_hbm.shape[1]
    half = blocks // 2
    rows = half * loads
    lanes = 2 * columns
    local_bits = blocks.bit_length() - 1
    tree_bits = local_bits + leaves.bit_length() - 1
    level_bits = [(tree_bits - 1 - level) % tree_bits for level in range(levels)]
    whole = whole_level(level_bits, local_bits)
    leaf = lax.axis_index("leaf")
    rank = lax.axis_index("rank")

    def partner_leaf(bit):
        step = 1 << (bit - local_bits)
        return leaf + step - 2 * step * ((leaf // step) % 2)

    def other_rank(away):
        return (rank + away) % ranks

    barrier = pltpu.get_barrier_semaphore()
    remote_bits = sorted({bit for bit in level_bits if bit >= local_bits})
    for away in range(1, ranks):
        pl.semaphore_signal(
            barrier, inc=1, device_id={"leaf": leaf, "rank": other_rank(away)}, device_id_type=MESH
        )
    for bit in remote_bits:
        for away in range(ranks):
            pl.semaphore_signal(
                barrier,
                inc=1,
                device_id={"leaf": partner_leaf(bit), "rank": other_rank(away)},
                device_id_type=MESH,
            )

    fetches = [
        pltpu.make_async_copy(order_hbm, order_ref, in_sem.at[0]),
        pltpu.make_async_copy(loads_hbm, loads_ref, in_sem.at[1]),
        pltpu.make_async_copy(present_hbm, present_ref, in_sem.at[2]),
    ]
    weight_fetches = [
        pltpu.make_async_copy(factors_hbm.at[level], weights.at[level], weight_sem.at[level])
        for level in range(levels)
    ]
    order_of_use = ([whole] if whole > 0 else []) + [level for level in range(levels) if level != whole]
    for fetch in fetches + [weight_fetches[level] for level in order_of_use]:
        fetch.start()
    for fetch in fetches:
        fetch.wait()

    lane = lax.broadcasted_iota(jnp.int32, (rows, lanes), 1)
    row = lax.broadcasted_iota(jnp.int32, (rows, lanes), 0)
    left = lane < columns

    def picks(block):
        wanted = lax.broadcasted_iota(jnp.int32, (width, width), 0)
        return jnp.where(order_ref[pl.ds(block, 1), :] == wanted, 1.0, 0.0).astype(jnp.bfloat16)

    def gathered(block):
        return jnp.dot(loads_ref[block], picks(block), preferred_element_type=jnp.float32)

    def packed(upper, lower):
        left = lax.broadcasted_iota(jnp.int32, (upper.shape[0], lanes), 1) < columns
        own, partner = [], []
        for tile in range(ranks // 2):
            a = upper[:, tile * lanes : (tile + 1) * lanes]
            b = lower[:, tile * lanes : (tile + 1) * lanes]
            a_moved = pltpu.roll(a, columns, 1)
            b_moved = pltpu.roll(b, columns, 1)
            own += [jnp.where(left, a, b_moved), jnp.where(left, a_moved, b)]
            partner += [jnp.where(left, b, a_moved), jnp.where(left, b_moved, a)]
        return own, partner

    def present_mask(level):
        def rows_of(first):
            mask = jnp.zeros((rows, lanes), jnp.float32)
            for at in range(half):
                value = present_ref[first + at, level].astype(jnp.float32)
                mask = jnp.where(row // loads == at, value, mask)
            return mask

        return jnp.where(left, rows_of(half), rows_of(0))

    def remote(level, src, slot, to_leaf, to_rank):
        return pltpu.make_async_remote_copy(
            src_ref=src,
            dst_ref=recv.at[level, slot],
            send_sem=send_sem.at[level],
            recv_sem=recv_sem.at[level],
            device_id={"leaf": to_leaf, "rank": to_rank},
            device_id_type=MESH,
        )

    sent = [0] * levels

    first = [gathered(block) for block in range(blocks)]
    own, partner = packed(
        jnp.concatenate(first[:half], axis=0), jnp.concatenate(first[half:], axis=0)
    )
    for at in range(ranks):
        send[0, 0, at] = own[at]
        send[0, 1, at] = partner[at]
    bulk = []
    if whole > 0:
        weight_fetches[whole].wait()
        for at in range(half):
            for side in range(2):
                pieces, _ = packed(
                    weights[whole, at, side].astype(jnp.float32),
                    weights[whole, half + at, side].astype(jnp.float32),
                )
                for to in range(ranks):
                    bulk_send[to, at, side] = pieces[to].astype(jnp.bfloat16)
        bulk_recv[rank] = bulk_send[rank]
        for away in range(1, ranks):
            bulk.append(
                pltpu.make_async_remote_copy(
                    src_ref=bulk_send.at[other_rank(away)],
                    dst_ref=bulk_recv.at[rank],
                    send_sem=bulk_sem.at[0],
                    recv_sem=bulk_sem.at[1],
                    device_id={"leaf": leaf, "rank": other_rank(away)},
                    device_id_type=MESH,
                )
            )
    pl.semaphore_wait(barrier, ranks - 1 + len(remote_bits) * ranks)
    if level_bits[0] >= local_bits:
        remote(0, send.at[0, 1, rank], ranks, partner_leaf(level_bits[0]), rank).start()
        sent[0] = 1
    for copy in bulk if whole == 1 else []:
        copy.start()

    for level in range(levels):
        bit = level_bits[level]
        if level == whole:
            all_rows = (blocks * loads, width)
            block_at = lax.broadcasted_iota(jnp.int32, all_rows, 0) // loads
            mask = jnp.zeros(all_rows, jnp.float32)
            for block in range(blocks):
                mask = jnp.where(
                    block_at == block, present_ref[block, level].astype(jnp.float32), mask
                )
            arrived = bulk_recv.at[pl.ds(0, ranks - 1)]
            pltpu.make_async_copy(arrived, arrived, bulk_sem.at[1]).wait()
            arrived = whole_recv.at[pl.ds(0, ranks - 1)]
            pltpu.make_async_copy(arrived, arrived, whole_sem.at[1]).wait()
            total = whole_recv[0].astype(jnp.float32)
            for at in range(1, ranks):
                total = total + whole_recv[at].astype(jnp.float32)
            other = jnp.concatenate([total[rows:], total[:rows]], axis=0) * mask
            spans, table = [], []
            for at in range(half):
                for side, value in enumerate((total, other)):
                    spans.append(jnp.where(block_at % half == at, value, 0.0).astype(jnp.bfloat16))
                    table += [bulk_recv[source, at, side] for source in range(ranks)]
            both = jnp.dot(
                jnp.concatenate(spans, axis=1),
                jnp.concatenate(table, axis=0),
                preferred_element_type=jnp.float32,
            )
            carried = jnp.where(left, both[:rows], both[rows:])
            continue
        mask = present_mask(level)
        if level == min(1, levels - 1):
            weight_fetches[levels - 1].wait()
            for block in range(blocks):
                wanted = picks(block)
                for side in range(2):
                    last_weights[block, side] = lax.dot_general(
                        weights[levels - 1, block, side],
                        wanted,
                        (((1,), (1,)), ((), ())),
                        preferred_element_type=jnp.float32,
                    ).astype(jnp.bfloat16)
        if level < levels - 1:
            weight_fetches[level].wait()
        if sent[level]:
            arrived = recv.at[level, pl.ds(0, sent[level])]
            pltpu.make_async_copy(arrived, arrived, recv_sem.at[level]).wait()
        if level == 0:
            state = send[0, 0, rank]
        elif level - 1 == whole:
            state = carried
        else:
            state = recv[level, 0]
            for at in range(1, ranks):
                state = state + recv[level, at]
        if bit >= local_bits:
            other = recv[level, ranks]
            if level > 0:
                for at in range(1, ranks):
                    other = other + recv[level, ranks + at]
        elif bit == local_bits - 1:
            other = state
        else:
            away = loads << bit
            moved = pltpu.roll(state, columns, 1)
            other = jnp.where(
                (row // away) % 2 == 0,
                pltpu.roll(moved, rows - away, 0),
                pltpu.roll(moved, away, 0),
            )
        other = other * mask
        upper = jnp.where(left, state, other)
        lower = jnp.where(left, other, state)

        def spread(piece):
            return jnp.concatenate(
                [jnp.where(row // loads == at, piece, 0.0) for at in range(half)], axis=1
            ).astype(jnp.bfloat16)

        table = weights.at[level] if level < levels - 1 else last_weights
        upper_weights = [table[at, side] for at in range(half) for side in (0, 1)]
        lower_weights = [table[half + at, side] for at in range(half) for side in (1, 0)]
        upper = jnp.dot(
            spread(upper),
            jnp.concatenate(upper_weights, axis=0),
            preferred_element_type=jnp.float32,
        )
        lower = jnp.dot(
            spread(lower),
            jnp.concatenate(lower_weights, axis=0),
            preferred_element_type=jnp.float32,
        )
        if level == levels - 1:
            break
        then = level + 1
        if then == whole:
            whole_send[...] = jnp.concatenate([upper, lower], axis=0).astype(jnp.bfloat16)
            for away in range(1, ranks):
                pltpu.make_async_remote_copy(
                    src_ref=whole_send,
                    dst_ref=whole_recv.at[rank],
                    send_sem=whole_sem.at[0],
                    recv_sem=whole_sem.at[1],
                    device_id={"leaf": leaf, "rank": other_rank(away)},
                    device_id_type=MESH,
                ).start()
            whole_recv[rank] = whole_send[...]
            continue
        own, partner = packed(upper, lower)
        with_partner = level_bits[then] >= local_bits
        for at in range(ranks):
            send[then, 0, at] = own[at]
            if with_partner:
                send[then, 1, at] = partner[at]
        for away in range(1, ranks):
            to = other_rank(away)
            remote(then, send.at[then, 0, to], rank, leaf, to).start()
            if with_partner:
                remote(
                    then, send.at[then, 1, to], ranks + rank, partner_leaf(level_bits[then]), to
                ).start()
        if with_partner:
            remote(
                then, send.at[then, 1, rank], ranks + rank, partner_leaf(level_bits[then]), rank
            ).start()
        sent[then] = ranks - 1 + (ranks if with_partner else 0)
        for copy in bulk if then == whole - 1 else []:
            copy.start()
        recv[then, rank] = send[then, 0, rank]

    last_send[...] = jnp.concatenate([upper, lower], axis=0).astype(jnp.bfloat16)
    lasts = [
        pltpu.make_async_remote_copy(
            src_ref=last_send,
            dst_ref=last_recv.at[rank],
            send_sem=last_send_sem,
            recv_sem=last_recv_sem,
            device_id={"leaf": leaf, "rank": other_rank(away)},
            device_id_type=MESH,
        )
        for away in range(1, ranks)
    ]
    for copy in lasts:
        copy.start()
    last_recv[rank] = last_send[...]
    for level in range(levels):
        if sent[level]:
            gone = recv.at[level, pl.ds(0, sent[level])]
            pltpu.make_async_copy(gone, gone, send_sem.at[level]).wait()
    if whole > 0:
        gone = bulk_recv.at[pl.ds(0, ranks - 1)]
        pltpu.make_async_copy(gone, gone, bulk_sem.at[0]).wait()
        gone = whole_recv.at[pl.ds(0, ranks - 1)]
        pltpu.make_async_copy(gone, gone, whole_sem.at[0]).wait()
    arrived = last_recv.at[pl.ds(0, ranks - 1)]
    pltpu.make_async_copy(arrived, arrived, last_recv_sem).wait()
    total = last_recv[0].astype(jnp.float32)
    for at in range(1, ranks):
        total = total + last_recv[at].astype(jnp.float32)
    for block in range(blocks):
        out_ref[block] = total[block * loads : (block + 1) * loads]
    pltpu.make_async_copy(arrived, arrived, last_send_sem).wait()


def local(leaves, ranks, load_vectors, cluster_order, block_present, factors):
    levels, blocks, _, columns, width = factors.shape
    loads = load_vectors.shape[1]
    rows = blocks // 2 * loads
    lanes = 2 * columns
    return pl.pallas_call(
        functools.partial(kernel, leaves, ranks),
        out_shape=jax.ShapeDtypeStruct((blocks, loads, width), jnp.float32),
        in_specs=[pl.BlockSpec(memory_space=pl.ANY)] * 4,
        out_specs=pl.BlockSpec(memory_space=pltpu.VMEM),
        scratch_shapes=[
            pltpu.VMEM(load_vectors.shape, load_vectors.dtype),
            pltpu.VMEM(cluster_order.shape, cluster_order.dtype),
            pltpu.SMEM(block_present.shape[::-1], block_present.dtype),
            pltpu.VMEM(factors.shape, factors.dtype),
            pltpu.VMEM(factors.shape[1:], factors.dtype),
            pltpu.VMEM((levels, 2, ranks, rows, lanes), jnp.float32),
            pltpu.VMEM((levels, 2 * ranks, rows, lanes), jnp.float32),
            pltpu.VMEM((blocks * loads, width), jnp.bfloat16),
            pltpu.VMEM((ranks, blocks * loads, width), jnp.bfloat16),
            pltpu.VMEM((blocks * loads, width), jnp.bfloat16),
            pltpu.VMEM((ranks, blocks * loads, width), jnp.bfloat16),
            pltpu.VMEM((ranks, blocks // 2, 2, columns, lanes), factors.dtype),
            pltpu.VMEM((ranks, blocks // 2, 2, columns, lanes), factors.dtype),
            pltpu.SemaphoreType.DMA((3,)),
            pltpu.SemaphoreType.DMA((levels,)),
            pltpu.SemaphoreType.DMA((levels,)),
            pltpu.SemaphoreType.DMA((levels,)),
            pltpu.SemaphoreType.DMA,
            pltpu.SemaphoreType.DMA,
            pltpu.SemaphoreType.DMA((2,)),
            pltpu.SemaphoreType.DMA((2,)),
        ],
        compiler_params=pltpu.CompilerParams(
            collective_id=0, has_side_effects=True, vmem_limit_bytes=VMEM_LIMIT
        ),
    )(load_vectors, cluster_order, block_present.T, factors)


def solution(mesh):
    in_specs = (
        P("leaf", None, None),
        P("leaf", None),
        P(None, "leaf"),
        P(None, "leaf", None, "rank", None),
    )
    return jax.shard_map(
        functools.partial(local, mesh.shape["leaf"], mesh.shape["rank"]),
        mesh=mesh,
        in_specs=in_specs,
        out_specs=P("leaf", None, None),
        check_vma=False,
    )
```

```python
import functools

import jax
import jax.numpy as jnp
from jax import lax
from jax.experimental import pallas as pl
from jax.experimental.pallas import tpu as pltpu
from jax.sharding import PartitionSpec as P

MESH = pl.DeviceIdType.MESH
BULK_LEAD = 2
VMEM_LIMIT = 63 * 1024 * 1024


def whole_levels(level_bits, local_bits):
    chosen = []
    for level in range(3, len(level_bits) - 1):
        near = level_bits[level + 1] <= local_bits and level_bits[level] >= local_bits - 1
        if near and level - 1 not in chosen:
            chosen.append(level)
    return chosen


def kernel(
    leaves,
    ranks,
    loads_hbm,
    order_hbm,
    present_hbm,
    factors_hbm,
    out_ref,
    loads_ref,
    order_ref,
    present_ref,
    weights,
    last_weights,
    send,
    recv,
    last_send,
    last_recv,
    whole_send,
    whole_recv,
    bulk_send,
    bulk_recv,
    in_sem,
    weight_sem,
    send_sem,
    recv_sem,
    last_send_sem,
    last_recv_sem,
    whole_sem,
    bulk_sem,
):
    levels, blocks, _, columns, width = factors_hbm.shape
    loads = loads_hbm.shape[1]
    half = blocks // 2
    rows = half * loads
    lanes = 2 * columns
    local_bits = blocks.bit_length() - 1
    tree_bits = local_bits + leaves.bit_length() - 1
    level_bits = [(tree_bits - 1 - level) % tree_bits for level in range(levels)]
    wholes = whole_levels(level_bits, local_bits)
    rounds = [level for level in range(1, levels) if level - 1 not in wholes]
    leaf = lax.axis_index("leaf")
    rank = lax.axis_index("rank")

    def partner_leaf(bit):
        step = 1 << (bit - local_bits)
        return leaf + step - 2 * step * ((leaf // step) % 2)

    def other_rank(away):
        return (rank + away) % ranks

    barrier = pltpu.get_barrier_semaphore()
    remote_bits = sorted({bit for bit in level_bits if bit >= local_bits})
    for away in range(1, ranks):
        pl.semaphore_signal(
            barrier, inc=1, device_id={"leaf": leaf, "rank": other_rank(away)}, device_id_type=MESH
        )
    for bit in remote_bits:
        for away in range(ranks):
            pl.semaphore_signal(
                barrier,
                inc=1,
                device_id={"leaf": partner_leaf(bit), "rank": other_rank(away)},
                device_id_type=MESH,
            )

    fetches = [
        pltpu.make_async_copy(order_hbm, order_ref, in_sem.at[0]),
        pltpu.make_async_copy(loads_hbm, loads_ref, in_sem.at[1]),
        pltpu.make_async_copy(present_hbm, present_ref, in_sem.at[2]),
    ]
    weight_fetches = [
        pltpu.make_async_copy(factors_hbm.at[level], weights.at[level], weight_sem.at[level])
        for level in range(levels)
    ]
    order_of_use = wholes[:1] + [level for level in range(levels) if level not in wholes[:1]]
    for fetch in fetches + [weight_fetches[level] for level in order_of_use]:
        fetch.start()
    for fetch in fetches:
        fetch.wait()

    lane = lax.broadcasted_iota(jnp.int32, (rows, lanes), 1)
    row = lax.broadcasted_iota(jnp.int32, (rows, lanes), 0)
    left = lane < columns

    def picks(block):
        wanted = lax.broadcasted_iota(jnp.int32, (width, width), 0)
        return jnp.where(order_ref[pl.ds(block, 1), :] == wanted, 1.0, 0.0).astype(jnp.bfloat16)

    def gathered(block):
        return jnp.dot(loads_ref[block], picks(block), preferred_element_type=jnp.float32)

    def packed(upper, lower):
        left = lax.broadcasted_iota(jnp.int32, (upper.shape[0], lanes), 1) < columns
        own, partner = [], []
        for tile in range(ranks // 2):
            a = upper[:, tile * lanes : (tile + 1) * lanes]
            b = lower[:, tile * lanes : (tile + 1) * lanes]
            a_moved = pltpu.roll(a, columns, 1)
            b_moved = pltpu.roll(b, columns, 1)
            own += [jnp.where(left, a, b_moved), jnp.where(left, a_moved, b)]
            partner += [jnp.where(left, b, a_moved), jnp.where(left, b_moved, a)]
        return own, partner

    def present_mask(level):
        def rows_of(first):
            mask = jnp.zeros((rows, lanes), jnp.float32)
            for at in range(half):
                value = present_ref[first + at, level].astype(jnp.float32)
                mask = jnp.where(row // loads == at, value, mask)
            return mask

        return jnp.where(left, rows_of(half), rows_of(0))

    def remote(level, src, slot, to_leaf, to_rank):
        return pltpu.make_async_remote_copy(
            src_ref=src,
            dst_ref=recv.at[level, slot],
            send_sem=send_sem.at[level],
            recv_sem=recv_sem.at[level],
            device_id={"leaf": to_leaf, "rank": to_rank},
            device_id_type=MESH,
        )

    sent = [0] * levels

    first = [gathered(block) for block in range(blocks)]
    own, partner = packed(
        jnp.concatenate(first[:half], axis=0), jnp.concatenate(first[half:], axis=0)
    )
    for at in range(ranks):
        send[0, 0, at] = own[at]
        send[0, 1, at] = partner[at]
    bulk = {level: [] for level in range(levels)}

    def prepare_bulk(at_whole):
        level = wholes[at_whole]
        weight_fetches[level].wait()
        before = rounds[: rounds.index(level)]
        for at in range(half):
            for side in range(2):
                pieces, _ = packed(
                    weights[level, at, side].astype(jnp.float32),
                    weights[level, half + at, side].astype(jnp.float32),
                )
                for to in range(ranks):
                    bulk_send[at_whole, to, at, side] = pieces[to].astype(jnp.bfloat16)
            for away in range(1, ranks):
                to = other_rank(away)
                bulk[before[max(at - BULK_LEAD, -len(before))]].append(
                    pltpu.make_async_remote_copy(
                        src_ref=bulk_send.at[at_whole, to, at],
                        dst_ref=bulk_recv.at[at_whole, rank, at],
                        send_sem=bulk_sem.at[at_whole, 0],
                        recv_sem=bulk_sem.at[at_whole, 1],
                        device_id={"leaf": leaf, "rank": to},
                        device_id_type=MESH,
                    )
                )
        bulk_recv[at_whole, rank] = bulk_send[at_whole, rank]

    for at_whole in range(len(wholes[:1])):
        prepare_bulk(at_whole)
    pl.semaphore_wait(barrier, ranks - 1 + len(remote_bits) * ranks)
    if level_bits[0] >= local_bits:
        remote(0, send.at[0, 1, rank], ranks, partner_leaf(level_bits[0]), rank).start()
        sent[0] = 1
    for at_whole in range(1, len(wholes)):
        prepare_bulk(at_whole)

    for level in range(levels):
        bit = level_bits[level]
        if level in wholes:
            at_whole = wholes.index(level)
            all_rows = (blocks * loads, width)
            block_at = lax.broadcasted_iota(jnp.int32, all_rows, 0) // loads
            mask = jnp.zeros(all_rows, jnp.float32)
            for block in range(blocks):
                mask = jnp.where(
                    block_at == block, present_ref[block, level].astype(jnp.float32), mask
                )
            arrived = bulk_recv.at[at_whole, pl.ds(0, ranks - 1)]
            pltpu.make_async_copy(arrived, arrived, bulk_sem.at[at_whole, 1]).wait()
            arrived = whole_recv.at[at_whole, pl.ds(0, sent[level])]
            pltpu.make_async_copy(arrived, arrived, whole_sem.at[at_whole, 1]).wait()

            def summed(first):
                result = whole_recv[at_whole, first].astype(jnp.float32)
                for at in range(1, ranks):
                    result = result + whole_recv[at_whole, first + at].astype(jnp.float32)
                return result

            total = summed(0)
            if bit >= local_bits:
                other = summed(ranks)
            else:
                other = jnp.concatenate([total[rows:], total[:rows]], axis=0)
            other = other * mask
            spans, table = [], []
            for at in range(half):
                for side, value in enumerate((total, other)):
                    spans.append(jnp.where(block_at % half == at, value, 0.0).astype(jnp.bfloat16))
                    table += [bulk_recv[at_whole, source, at, side] for source in range(ranks)]
            both = jnp.dot(
                jnp.concatenate(spans, axis=1),
                jnp.concatenate(table, axis=0),
                preferred_element_type=jnp.float32,
            )
            carried = jnp.where(left, both[:rows], both[rows:])
            then = level + 1
            if level_bits[then] >= local_bits:
                send[then, 1, 0] = pltpu.roll(carried, columns, 1)
                remote(
                    then, send.at[then, 1, 0], ranks, partner_leaf(level_bits[then]), rank
                ).start()
                sent[then] = 1
            continue
        mask = present_mask(level)
        if level == min(1, levels - 1):
            weight_fetches[levels - 1].wait()
            for block in range(blocks):
                wanted = picks(block)
                for side in range(2):
                    last_weights[block, side] = lax.dot_general(
                        weights[levels - 1, block, side],
                        wanted,
                        (((1,), (1,)), ((), ())),
                        preferred_element_type=jnp.float32,
                    ).astype(jnp.bfloat16)
        if level < levels - 1:
            weight_fetches[level].wait()
        if sent[level]:
            arrived = recv.at[level, pl.ds(0, sent[level])]
            pltpu.make_async_copy(arrived, arrived, recv_sem.at[level]).wait()
        if level == 0:
            state = send[0, 0, rank]
        elif level - 1 in wholes:
            state = carried
        else:
            state = recv[level, 0]
            for at in range(1, ranks):
                state = state + recv[level, at]
        if bit >= local_bits:
            other = recv[level, ranks]
            if level > 0 and level - 1 not in wholes:
                for at in range(1, ranks):
                    other = other + recv[level, ranks + at]
        elif bit == local_bits - 1:
            other = state
        else:
            away = loads << bit
            moved = pltpu.roll(state, columns, 1)
            other = jnp.where(
                (row // away) % 2 == 0,
                pltpu.roll(moved, rows - away, 0),
                pltpu.roll(moved, away, 0),
            )
        other = other * mask
        upper = jnp.where(left, state, other)
        lower = jnp.where(left, other, state)

        def spread(piece):
            return jnp.concatenate(
                [jnp.where(row // loads == at, piece, 0.0) for at in range(half)], axis=1
            ).astype(jnp.bfloat16)

        table = weights.at[level] if level < levels - 1 else last_weights
        upper_weights = [table[at, side] for at in range(half) for side in (0, 1)]
        lower_weights = [table[half + at, side] for at in range(half) for side in (1, 0)]
        upper = jnp.dot(
            spread(upper),
            jnp.concatenate(upper_weights, axis=0),
            preferred_element_type=jnp.float32,
        )
        lower = jnp.dot(
            spread(lower),
            jnp.concatenate(lower_weights, axis=0),
            preferred_element_type=jnp.float32,
        )
        if level == levels - 1:
            break
        then = level + 1
        with_partner = level_bits[then] >= local_bits
        sent[then] = ranks - 1 + (ranks if with_partner else 0)
        if then in wholes:
            at_whole = wholes.index(then)
            whole_send[at_whole] = jnp.concatenate([upper, lower], axis=0).astype(jnp.bfloat16)

            def send_whole(slot, to_leaf, to_rank):
                pltpu.make_async_remote_copy(
                    src_ref=whole_send.at[at_whole],
                    dst_ref=whole_recv.at[at_whole, slot],
                    send_sem=whole_sem.at[at_whole, 0],
                    recv_sem=whole_sem.at[at_whole, 1],
                    device_id={"leaf": to_leaf, "rank": to_rank},
                    device_id_type=MESH,
                ).start()

            for away in range(1, ranks):
                send_whole(rank, leaf, other_rank(away))
                if with_partner:
                    send_whole(
                        ranks + rank, partner_leaf(level_bits[then]), other_rank(away)
                    )
            if with_partner:
                send_whole(ranks + rank, partner_leaf(level_bits[then]), rank)
            for copy in bulk[then]:
                copy.start()
            whole_recv[at_whole, rank] = whole_send[at_whole]
            continue
        own, partner = packed(upper, lower)
        for at in range(ranks):
            send[then, 0, at] = own[at]
            if with_partner:
                send[then, 1, at] = partner[at]
        for away in range(1, ranks):
            to = other_rank(away)
            remote(then, send.at[then, 0, to], rank, leaf, to).start()
            if with_partner:
                remote(
                    then, send.at[then, 1, to], ranks + rank, partner_leaf(level_bits[then]), to
                ).start()
        if with_partner:
            remote(
                then, send.at[then, 1, rank], ranks + rank, partner_leaf(level_bits[then]), rank
            ).start()
        for copy in bulk[then]:
            copy.start()
        recv[then, rank] = send[then, 0, rank]

    last_send[...] = jnp.concatenate([upper, lower], axis=0).astype(jnp.bfloat16)
    lasts = [
        pltpu.make_async_remote_copy(
            src_ref=last_send,
            dst_ref=last_recv.at[rank],
            send_sem=last_send_sem,
            recv_sem=last_recv_sem,
            device_id={"leaf": leaf, "rank": other_rank(away)},
            device_id_type=MESH,
        )
        for away in range(1, ranks)
    ]
    for copy in lasts:
        copy.start()
    last_recv[rank] = last_send[...]
    for level in range(levels):
        if sent[level] and level not in wholes:
            gone = recv.at[level, pl.ds(0, sent[level])]
            pltpu.make_async_copy(gone, gone, send_sem.at[level]).wait()
    for at_whole, level in enumerate(wholes):
        gone = bulk_recv.at[at_whole, pl.ds(0, ranks - 1)]
        pltpu.make_async_copy(gone, gone, bulk_sem.at[at_whole, 0]).wait()
        gone = whole_recv.at[at_whole, pl.ds(0, sent[level])]
        pltpu.make_async_copy(gone, gone, whole_sem.at[at_whole, 0]).wait()
    arrived = last_recv.at[pl.ds(0, ranks - 1)]
    pltpu.make_async_copy(arrived, arrived, last_recv_sem).wait()
    total = last_recv[0].astype(jnp.float32)
    for at in range(1, ranks):
        total = total + last_recv[at].astype(jnp.float32)
    for block in range(blocks):
        out_ref[block] = total[block * loads : (block + 1) * loads]
    pltpu.make_async_copy(arrived, arrived, last_send_sem).wait()


def local(leaves, ranks, load_vectors, cluster_order, block_present, factors):
    levels, blocks, _, columns, width = factors.shape
    loads = load_vectors.shape[1]
    rows = blocks // 2 * loads
    lanes = 2 * columns
    return pl.pallas_call(
        functools.partial(kernel, leaves, ranks),
        out_shape=pltpu.VMEM((blocks, loads, width), jnp.float32),
        in_specs=[pl.BlockSpec(memory_space=pl.ANY)] * 4,
        out_specs=pl.BlockSpec(memory_space=pltpu.VMEM),
        scratch_shapes=[
            pltpu.VMEM(load_vectors.shape, load_vectors.dtype),
            pltpu.VMEM(cluster_order.shape, cluster_order.dtype),
            pltpu.SMEM(block_present.shape[::-1], block_present.dtype),
            pltpu.VMEM(factors.shape, factors.dtype),
            pltpu.VMEM(factors.shape[1:], factors.dtype),
            pltpu.VMEM((levels, 2, ranks, rows, lanes), jnp.float32),
            pltpu.VMEM((levels, 2 * ranks, rows, lanes), jnp.float32),
            pltpu.VMEM((blocks * loads, width), jnp.bfloat16),
            pltpu.VMEM((ranks, blocks * loads, width), jnp.bfloat16),
            pltpu.VMEM((levels, blocks * loads, width), jnp.bfloat16),
            pltpu.VMEM((levels, 2 * ranks, blocks * loads, width), jnp.bfloat16),
            pltpu.VMEM((levels, ranks, blocks // 2, 2, columns, lanes), factors.dtype),
            pltpu.VMEM((levels, ranks, blocks // 2, 2, columns, lanes), factors.dtype),
            pltpu.SemaphoreType.DMA((3,)),
            pltpu.SemaphoreType.DMA((levels,)),
            pltpu.SemaphoreType.DMA((levels,)),
            pltpu.SemaphoreType.DMA((levels,)),
            pltpu.SemaphoreType.DMA,
            pltpu.SemaphoreType.DMA,
            pltpu.SemaphoreType.DMA((levels, 2)),
            pltpu.SemaphoreType.DMA((levels, 2)),
        ],
        compiler_params=pltpu.CompilerParams(
            collective_id=0, has_side_effects=True, vmem_limit_bytes=VMEM_LIMIT
        ),
    )(load_vectors, cluster_order, block_present.T, factors)


def solution(mesh):
    in_specs = (
        P("leaf", None, None),
        P("leaf", None),
        P(None, "leaf"),
        P(None, "leaf", None, "rank", None),
    )
    return jax.shard_map(
        functools.partial(local, mesh.shape["leaf"], mesh.shape["rank"]),
        mesh=mesh,
        in_specs=in_specs,
        out_specs=P("leaf", None, None),
        check_vma=False,
    )
```

```python
import functools

import jax
import jax.numpy as jnp
from jax import lax
from jax.experimental import pallas as pl
from jax.experimental.pallas import tpu as pltpu
from jax.sharding import PartitionSpec as P

MESH = pl.DeviceIdType.MESH
BULK_LEAD = 2
VMEM_LIMIT = 63 * 1024 * 1024


def whole_levels(level_bits, local_bits):
    chosen = []
    for level in range(3, len(level_bits) - 1):
        near = level_bits[level + 1] <= local_bits and level_bits[level] >= local_bits - 1
        if near and level - 1 not in chosen:
            chosen.append(level)
    return chosen


def kernel(
    leaves,
    ranks,
    loads_hbm,
    order_hbm,
    present_hbm,
    factors_hbm,
    out_ref,
    loads_ref,
    order_ref,
    present_ref,
    weights,
    last_weights,
    send,
    recv,
    last_send,
    last_recv,
    whole_send,
    whole_recv,
    bulk_send,
    bulk_recv,
    in_sem,
    weight_sem,
    send_sem,
    recv_sem,
    last_send_sem,
    last_recv_sem,
    whole_sem,
    bulk_sem,
):
    levels, blocks, _, columns, width = factors_hbm.shape
    loads = loads_hbm.shape[1]
    half = blocks // 2
    rows = half * loads
    lanes = 2 * columns
    local_bits = blocks.bit_length() - 1
    tree_bits = local_bits + leaves.bit_length() - 1
    level_bits = [(tree_bits - 1 - level) % tree_bits for level in range(levels)]
    wholes = whole_levels(level_bits, local_bits)
    rounds = [level for level in range(1, levels) if level - 1 not in wholes]
    leaf = lax.axis_index("leaf")
    rank = lax.axis_index("rank")

    def partner_leaf(bit):
        step = 1 << (bit - local_bits)
        return leaf + step - 2 * step * ((leaf // step) % 2)

    def other_rank(away):
        bit = ranks - away
        to = rank
        step = 1
        while step < ranks:
            if bit // step % 2:
                to = to + step - 2 * step * ((rank // step) % 2)
            step *= 2
        return to

    barrier = pltpu.get_barrier_semaphore()
    remote_bits = sorted({bit for bit in level_bits if bit >= local_bits})
    for bit in remote_bits:
        for away in range(1, ranks + 1):
            pl.semaphore_signal(
                barrier,
                inc=1,
                device_id={"leaf": partner_leaf(bit), "rank": other_rank(away)},
                device_id_type=MESH,
            )

    for away in range(1, ranks):
        pl.semaphore_signal(
            barrier, inc=1, device_id={"leaf": leaf, "rank": other_rank(away)}, device_id_type=MESH
        )
    fetches = [
        pltpu.make_async_copy(order_hbm, order_ref, in_sem.at[0]),
        pltpu.make_async_copy(loads_hbm, loads_ref, in_sem.at[1]),
        pltpu.make_async_copy(present_hbm, present_ref, in_sem.at[2]),
    ]
    weight_fetches = [
        pltpu.make_async_copy(factors_hbm.at[level], weights.at[level], weight_sem.at[level])
        for level in range(levels)
    ]
    order_of_use = wholes[:1] + [level for level in range(levels) if level not in wholes[:1]]
    for fetch in fetches + [weight_fetches[level] for level in order_of_use]:
        fetch.start()
    for fetch in fetches:
        fetch.wait()

    lane = lax.broadcasted_iota(jnp.int32, (rows, lanes), 1)
    row = lax.broadcasted_iota(jnp.int32, (rows, lanes), 0)
    left = lane < columns

    def picks(block):
        wanted = lax.broadcasted_iota(jnp.int32, (width, width), 0)
        return jnp.where(order_ref[pl.ds(block, 1), :] == wanted, 1.0, 0.0).astype(jnp.bfloat16)

    def gathered(block):
        return jnp.dot(loads_ref[block], picks(block), preferred_element_type=jnp.float32)

    def packed(upper, lower):
        left = lax.broadcasted_iota(jnp.int32, (upper.shape[0], lanes), 1) < columns
        own, partner = [], []
        for tile in range(ranks // 2):
            a = upper[:, tile * lanes : (tile + 1) * lanes]
            b = lower[:, tile * lanes : (tile + 1) * lanes]
            a_moved = pltpu.roll(a, columns, 1)
            b_moved = pltpu.roll(b, columns, 1)
            own += [jnp.where(left, a, b_moved), jnp.where(left, a_moved, b)]
            partner += [jnp.where(left, b, a_moved), jnp.where(left, b_moved, a)]
        return own, partner

    def present_mask(level):
        def rows_of(first):
            mask = jnp.zeros((rows, lanes), jnp.float32)
            for at in range(half):
                value = present_ref[first + at, level].astype(jnp.float32)
                mask = jnp.where(row // loads == at, value, mask)
            return mask

        return jnp.where(left, rows_of(half), rows_of(0))

    def remote(level, src, slot, to_leaf, to_rank):
        return pltpu.make_async_remote_copy(
            src_ref=src,
            dst_ref=recv.at[level, slot],
            send_sem=send_sem.at[level],
            recv_sem=recv_sem.at[level],
            device_id={"leaf": to_leaf, "rank": to_rank},
            device_id_type=MESH,
        )

    sent = [0] * levels

    first = [gathered(block) for block in range(blocks)]
    own, partner = packed(
        jnp.concatenate(first[:half], axis=0), jnp.concatenate(first[half:], axis=0)
    )
    for at in range(ranks):
        send[0, 0, at] = own[at]
        send[0, 1, at] = partner[at]
    bulk = {level: [] for level in range(levels)}

    def prepare_bulk(at_whole):
        level = wholes[at_whole]
        weight_fetches[level].wait()
        before = rounds[: rounds.index(level)]
        for at in range(half):
            for side in range(2):
                pieces, _ = packed(
                    weights[level, at, side].astype(jnp.float32),
                    weights[level, half + at, side].astype(jnp.float32),
                )
                for to in range(ranks):
                    bulk_send[at_whole, to, at, side] = pieces[to].astype(jnp.bfloat16)
            for away in range(1, ranks):
                to = other_rank(away)
                bulk[before[max(at - BULK_LEAD, -len(before))]].append(
                    pltpu.make_async_remote_copy(
                        src_ref=bulk_send.at[at_whole, to, at],
                        dst_ref=bulk_recv.at[at_whole, rank, at],
                        send_sem=bulk_sem.at[at_whole, 0],
                        recv_sem=bulk_sem.at[at_whole, 1],
                        device_id={"leaf": leaf, "rank": to},
                        device_id_type=MESH,
                    )
                )
        bulk_recv[at_whole, rank] = bulk_send[at_whole, rank]

    for at_whole in range(len(wholes[:1])):
        prepare_bulk(at_whole)
    pl.semaphore_wait(barrier, ranks - 1 + len(remote_bits) * ranks)
    if level_bits[0] >= local_bits:
        remote(0, send.at[0, 1, rank], ranks, partner_leaf(level_bits[0]), rank).start()
        sent[0] = 1
    for at_whole in range(1, len(wholes)):
        prepare_bulk(at_whole)

    for level in range(levels):
        bit = level_bits[level]
        if level in wholes:
            at_whole = wholes.index(level)
            all_rows = (blocks * loads, width)
            block_at = lax.broadcasted_iota(jnp.int32, all_rows, 0) // loads
            mask = jnp.zeros(all_rows, jnp.float32)
            for block in range(blocks):
                mask = jnp.where(
                    block_at == block, present_ref[block, level].astype(jnp.float32), mask
                )
            arrived = bulk_recv.at[at_whole, pl.ds(0, ranks - 1)]
            pltpu.make_async_copy(arrived, arrived, bulk_sem.at[at_whole, 1]).wait()
            arrived = whole_recv.at[at_whole, pl.ds(0, sent[level])]
            pltpu.make_async_copy(arrived, arrived, whole_sem.at[at_whole, 1]).wait()

            def summed(first):
                result = whole_recv[at_whole, first].astype(jnp.float32)
                for at in range(1, ranks):
                    result = result + whole_recv[at_whole, first + at].astype(jnp.float32)
                return result

            total = summed(0)
            if bit >= local_bits:
                other = summed(ranks)
            else:
                other = jnp.concatenate([total[rows:], total[:rows]], axis=0)
            other = other * mask
            spans, table = [], []
            for at in range(half):
                for side, value in enumerate((total, other)):
                    spans.append(jnp.where(block_at % half == at, value, 0.0).astype(jnp.bfloat16))
                    table += [bulk_recv[at_whole, source, at, side] for source in range(ranks)]
            both = jnp.dot(
                jnp.concatenate(spans, axis=1),
                jnp.concatenate(table, axis=0),
                preferred_element_type=jnp.float32,
            )
            carried = jnp.where(left, both[:rows], both[rows:])
            then = level + 1
            if level_bits[then] >= local_bits:
                send[then, 1, 0] = pltpu.roll(carried, columns, 1)
                remote(
                    then, send.at[then, 1, 0], ranks, partner_leaf(level_bits[then]), rank
                ).start()
                sent[then] = 1
            continue
        mask = present_mask(level)
        if level == min(1, levels - 1):
            weight_fetches[levels - 1].wait()
            for block in range(blocks):
                wanted = picks(block)
                for side in range(2):
                    last_weights[block, side] = lax.dot_general(
                        weights[levels - 1, block, side],
                        wanted,
                        (((1,), (1,)), ((), ())),
                        preferred_element_type=jnp.float32,
                    ).astype(jnp.bfloat16)
        if level < levels - 1:
            weight_fetches[level].wait()
        if sent[level]:
            arrived = recv.at[level, pl.ds(0, sent[level])]
            pltpu.make_async_copy(arrived, arrived, recv_sem.at[level]).wait()
        if level == 0:
            state = send[0, 0, rank]
        elif level - 1 in wholes:
            state = carried
        else:
            state = recv[level, 0]
            for at in range(1, ranks):
                state = state + recv[level, at]
        if bit >= local_bits:
            other = recv[level, ranks]
            if level > 0 and level - 1 not in wholes:
                for at in range(1, ranks):
                    other = other + recv[level, ranks + at]
        elif bit == local_bits - 1:
            other = state
        else:
            away = loads << bit
            moved = pltpu.roll(state, columns, 1)
            other = jnp.where(
                (row // away) % 2 == 0,
                pltpu.roll(moved, rows - away, 0),
                pltpu.roll(moved, away, 0),
            )
        other = other * mask
        upper = jnp.where(left, state, other)
        lower = jnp.where(left, other, state)

        def spread(piece):
            return jnp.concatenate(
                [jnp.where(row // loads == at, piece, 0.0) for at in range(half)], axis=1
            ).astype(jnp.bfloat16)

        table = weights.at[level] if level < levels - 1 else last_weights
        upper_weights = [table[at, side] for at in range(half) for side in (0, 1)]
        lower_weights = [table[half + at, side] for at in range(half) for side in (1, 0)]
        upper = jnp.dot(
            spread(upper),
            jnp.concatenate(upper_weights, axis=0),
            preferred_element_type=jnp.float32,
        )
        lower = jnp.dot(
            spread(lower),
            jnp.concatenate(lower_weights, axis=0),
            preferred_element_type=jnp.float32,
        )
        if level == levels - 1:
            break
        then = level + 1
        with_partner = level_bits[then] >= local_bits
        sent[then] = ranks - 1 + (ranks if with_partner else 0)
        if then in wholes:
            at_whole = wholes.index(then)
            whole_send[at_whole] = jnp.concatenate([upper, lower], axis=0).astype(jnp.bfloat16)

            def send_whole(slot, to_leaf, to_rank):
                pltpu.make_async_remote_copy(
                    src_ref=whole_send.at[at_whole],
                    dst_ref=whole_recv.at[at_whole, slot],
                    send_sem=whole_sem.at[at_whole, 0],
                    recv_sem=whole_sem.at[at_whole, 1],
                    device_id={"leaf": to_leaf, "rank": to_rank},
                    device_id_type=MESH,
                ).start()

            for away in range(1, ranks):
                if with_partner:
                    send_whole(
                        ranks + rank, partner_leaf(level_bits[then]), other_rank(away)
                    )
                send_whole(rank, leaf, other_rank(away))
            if with_partner:
                send_whole(ranks + rank, partner_leaf(level_bits[then]), rank)
            for copy in bulk[then]:
                copy.start()
            whole_recv[at_whole, rank] = whole_send[at_whole]
            continue
        own, partner = packed(upper, lower)
        for at in range(ranks):
            send[then, 0, at] = own[at]
            if with_partner:
                send[then, 1, at] = partner[at]
        for away in range(1, ranks):
            to = other_rank(away)
            if with_partner:
                remote(
                    then, send.at[then, 1, to], ranks + rank, partner_leaf(level_bits[then]), to
                ).start()
            remote(then, send.at[then, 0, to], rank, leaf, to).start()
        if with_partner:
            remote(
                then, send.at[then, 1, rank], ranks + rank, partner_leaf(level_bits[then]), rank
            ).start()
        for copy in bulk[then]:
            copy.start()
        recv[then, rank] = send[then, 0, rank]

    last_send[...] = jnp.concatenate([upper, lower], axis=0).astype(jnp.bfloat16)
    lasts = [
        pltpu.make_async_remote_copy(
            src_ref=last_send,
            dst_ref=last_recv.at[rank],
            send_sem=last_send_sem,
            recv_sem=last_recv_sem,
            device_id={"leaf": leaf, "rank": other_rank(away)},
            device_id_type=MESH,
        )
        for away in range(1, ranks)
    ]
    for copy in lasts:
        copy.start()
    last_recv[rank] = last_send[...]
    for level in range(levels):
        if sent[level] and level not in wholes:
            gone = recv.at[level, pl.ds(0, sent[level])]
            pltpu.make_async_copy(gone, gone, send_sem.at[level]).wait()
    for at_whole, level in enumerate(wholes):
        gone = bulk_recv.at[at_whole, pl.ds(0, ranks - 1)]
        pltpu.make_async_copy(gone, gone, bulk_sem.at[at_whole, 0]).wait()
        gone = whole_recv.at[at_whole, pl.ds(0, sent[level])]
        pltpu.make_async_copy(gone, gone, whole_sem.at[at_whole, 0]).wait()
    arrived = last_recv.at[pl.ds(0, ranks - 1)]
    pltpu.make_async_copy(arrived, arrived, last_recv_sem).wait()
    total = last_recv[0].astype(jnp.float32)
    for at in range(1, ranks):
        total = total + last_recv[at].astype(jnp.float32)
    for block in range(blocks):
        out_ref[block] = total[block * loads : (block + 1) * loads]
    pltpu.make_async_copy(arrived, arrived, last_send_sem).wait()


def local(leaves, ranks, load_vectors, cluster_order, block_present, factors):
    levels, blocks, _, columns, width = factors.shape
    loads = load_vectors.shape[1]
    rows = blocks // 2 * loads
    lanes = 2 * columns
    return pl.pallas_call(
        functools.partial(kernel, leaves, ranks),
        out_shape=pltpu.VMEM((blocks, loads, width), jnp.float32),
        in_specs=[pl.BlockSpec(memory_space=pl.ANY)] * 4,
        out_specs=pl.BlockSpec(memory_space=pltpu.VMEM),
        scratch_shapes=[
            pltpu.VMEM(load_vectors.shape, load_vectors.dtype),
            pltpu.VMEM(cluster_order.shape, cluster_order.dtype),
            pltpu.SMEM(block_present.shape[::-1], block_present.dtype),
            pltpu.VMEM(factors.shape, factors.dtype),
            pltpu.VMEM(factors.shape[1:], factors.dtype),
            pltpu.VMEM((levels, 2, ranks, rows, lanes), jnp.float32),
            pltpu.VMEM((levels, 2 * ranks, rows, lanes), jnp.float32),
            pltpu.VMEM((blocks * loads, width), jnp.bfloat16),
            pltpu.VMEM((ranks, blocks * loads, width), jnp.bfloat16),
            pltpu.VMEM((levels, blocks * loads, width), jnp.bfloat16),
            pltpu.VMEM((levels, 2 * ranks, blocks * loads, width), jnp.bfloat16),
            pltpu.VMEM((levels, ranks, blocks // 2, 2, columns, lanes), factors.dtype),
            pltpu.VMEM((levels, ranks, blocks // 2, 2, columns, lanes), factors.dtype),
            pltpu.SemaphoreType.DMA((3,)),
            pltpu.SemaphoreType.DMA((levels,)),
            pltpu.SemaphoreType.DMA((levels,)),
            pltpu.SemaphoreType.DMA((levels,)),
            pltpu.SemaphoreType.DMA,
            pltpu.SemaphoreType.DMA,
            pltpu.SemaphoreType.DMA((levels, 2)),
            pltpu.SemaphoreType.DMA((levels, 2)),
        ],
        compiler_params=pltpu.CompilerParams(
            collective_id=0, has_side_effects=True, vmem_limit_bytes=VMEM_LIMIT
        ),
    )(load_vectors, cluster_order, block_present.T, factors)


def solution(mesh):
    in_specs = (
        P("leaf", None, None),
        P("leaf", None),
        P(None, "leaf"),
        P(None, "leaf", None, "rank", None),
    )
    return jax.shard_map(
        functools.partial(local, mesh.shape["leaf"], mesh.shape["rank"]),
        mesh=mesh,
        in_specs=in_specs,
        out_specs=P("leaf", None, None),
        check_vma=False,
    )
```
